256 devices in a mesh: leaf: 16 (over y_hi, z), panel: 16 (over x, y_lo, core).
Axes of the slice: x: 4, y: 4 (y_hi: 2, y_lo: 2; y = y_hi * 2 + y_lo), z: 8, core: 2. Of those that a mesh axis runs over, the one named last changes fastest.
Arguments:
- a21: bfloat16 [16, 16384, 256], P('leaf', 'panel'), may hold values from -1.5 to 1.5
- l11_inv: bfloat16 [16, 256, 256], P('leaf'), as said below
- a22: bfloat16 [16, 16384, 2048], P('leaf', 'panel'), may hold values from -6 to 6
- tasks: int32 [16, 128], P('leaf', 'panel'), may hold values from 0 to 16
- emap: int32 [16, 128], P('leaf', 'panel'), may hold values from 0 to 7, as said below
- parent_in: float32 [16384, 2048], P('panel', 'leaf'), may hold values from -6 to 6
Outputs:
- l21: bfloat16 [16, 16384, 256], P('leaf', 'panel')
- parent_out: float32 [16384, 2048], P('panel', 'leaf')
The draws below stay inside these ranges and needn't reach their ends.
Inputs may be any that keep to these rules, and one draw needn't show every extreme that they name: `l11_inv`: lower triangular with positive diagonal. `emap`: the 8 row tiles of one front on one device go to the 8 parent tiles of that device in some order (a permutation of 0 to 7).
All inputs are finite; a program needn't handle non-finite values.
Results may differ from the reference program's by a relative error of at most 0.017.
Values may be sent and summed in bfloat16 or wider, within the bound.
No kernel may reach another device: no remote copies, remote signals or barrier semaphores. Data moves between devices by JAX's collectives and lax.ppermute only.
A program may use at most 64 MiB of HBM per device.

```python
import jax
import jax.numpy as jnp
from jax import lax

PW = 256
TILE = 128
ROWS_DEV = 1024
WIN_DEV = 128
PT_DEV = 8
FRONTS = 16
ROWS = 16384
WIN = 2048
PROWS = 16384
N_PANEL = 16


def draw_l11_inv(key, part):
    key = jax.random.fold_in(key, 5)
    first, second = jax.random.split(key)
    offdiag = jax.random.normal(first, (FRONTS, PW, PW), jnp.float32)
    diagvals = jax.random.uniform(second, (FRONTS, PW, 1), jnp.float32, 0.5, 2.0)
    rowsidx = jnp.arange(PW)[:, None]
    colsidx = jnp.arange(PW)[None, :]
    lower = jnp.where(rowsidx > colsidx, offdiag * (0.8 / PW ** 0.5), 0.0)
    return (lower + jnp.where(rowsidx == colsidx, diagvals, 0.0)).astype(jnp.bfloat16)


def draw_tasks(key, part):
    key = jax.random.fold_in(key, 11)
    first, second, third = jax.random.split(key, 3)
    tiles_all = ROWS // TILE
    highest = WIN // TILE
    order = jax.random.permutation(first, FRONTS)
    level = 1 + ((order + 1) * highest - 1) // FRONTS
    counts = jax.random.randint(second, (FRONTS, tiles_all), 0, highest + 1)
    counts = jnp.minimum(counts, level[:, None])
    chosen = jax.random.randint(third, (FRONTS,), 0, tiles_all)
    counts = jnp.where(jnp.arange(tiles_all)[None, :] == chosen[:, None], level[:, None], counts)
    return counts.astype(jnp.int32)


def draw_emap(key, part):
    key = jax.random.fold_in(key, 17)
    first, second = jax.random.split(key)
    per_block = ROWS_DEV // TILE
    blocks = FRONTS * N_PANEL
    shuffled = jax.vmap(lambda sub: jax.random.permutation(sub, PT_DEV))(jax.random.split(first, blocks))
    ends = (shuffled == 0) | (shuffled == PT_DEV - 1)
    priority = jnp.where(ends, -1, jnp.arange(PT_DEV)[None, :]).astype(jnp.int32)
    ranking = jnp.argsort(priority, axis=1, stable=True)
    chosen = jnp.take_along_axis(shuffled, ranking, axis=1)[:, :per_block]
    mixing = jax.vmap(lambda sub: jax.random.permutation(sub, per_block))(jax.random.split(second, blocks))
    result = jnp.take_along_axis(chosen, mixing, axis=1)
    return result.reshape(FRONTS, N_PANEL * per_block).astype(jnp.int32)


def shard_levels(own_key, extent, pieces, smallest, largest):
    def one(dim, blocks):
        heights = jax.random.uniform(jax.random.fold_in(jax.random.fold_in(own_key, 6), dim), (blocks,), jnp.float32, smallest / len(pieces), largest / len(pieces))
        return jnp.repeat(jnp.exp(heights), extent[dim] // blocks).reshape((-1,) + (1,) * (len(extent) - dim - 1))

    factor_of = one(*pieces[0])
    for cut in pieces[1:]:
        factor_of = factor_of * one(*cut)
    return factor_of


def gaussian(stream_key, dims, scale, reach, cuts=(), dtype=jnp.bfloat16):
    array = scale * jax.random.normal(stream_key, dims, jnp.float32)
    if cuts:
        array = array * shard_levels(stream_key, dims, cuts, -0.22, 0.18)
    return jnp.clip(array, -reach, reach).astype(dtype)


def setup_inputs(seed: int = 0) -> dict:
    arg_keys = jax.random.split(jax.random.key(seed), 7)
    return {
        "a21": gaussian(arg_keys[0], (FRONTS, ROWS, PW), 0.25, 1.5, ((0, 16), (1, 16))),
        "l11_inv": draw_l11_inv(jax.random.fold_in(arg_keys[6], 71), 0),
        "a22": gaussian(arg_keys[2], (FRONTS, ROWS, WIN), 1.0, 6.0, ((0, 16), (1, 16))),
        "tasks": draw_tasks(jax.random.fold_in(arg_keys[6], 71), 0),
        "emap": draw_emap(jax.random.fold_in(arg_keys[6], 71), 0),
        "parent_in": gaussian(arg_keys[5], (PROWS, WIN), 1.0, 6.0, ((0, 16), (1, 16)), jnp.float32),
    }


def reference(a21, l11_inv, a22, tasks, emap, parent_in):
    tiles_dev = ROWS_DEV // TILE

    def front_step(parent, inputs):
        panel_rows, inverse, trailing, counts, row_maps = inputs
        factor = jnp.dot(panel_rows, inverse.T, preferred_element_type=jnp.float32).astype(jnp.bfloat16)
        window = factor.reshape(N_PANEL, ROWS_DEV, PW)[:, :WIN_DEV].reshape(WIN, PW)
        update = jnp.dot(factor, window.T, preferred_element_type=jnp.float32)
        limits = jnp.repeat(counts * TILE, TILE)
        columns = jnp.arange(WIN)
        planned = columns[None, :] < limits[:, None]
        widened = trailing.astype(jnp.float32)
        contribution = jnp.where(planned, widened - update, widened).astype(jnp.bfloat16)
        tile_blocks = contribution.reshape(N_PANEL, tiles_dev, TILE, WIN).astype(jnp.float32)
        onehot = (row_maps.reshape(N_PANEL, tiles_dev)[:, :, None] == jnp.arange(PT_DEV)[None, None, :]).astype(jnp.float32)
        placed = jnp.einsum("ptk,ptrw->pkrw", onehot, tile_blocks)
        return parent + placed.reshape(PROWS, WIN), factor

    parent, factors = lax.scan(front_step, parent_in, (a21, l11_inv, a22, tasks, emap))
    return factors, parent
```

```python
import jax
import jax.numpy as jnp
from jax import lax
from jax.experimental import pallas as pl
from jax.experimental.pallas import tpu as pltpu
from jax.sharding import PartitionSpec as P

TILE = 128
TILES_DEV = 8
ROWS_DEV = TILES_DEV * TILE
PW = 256
STREAMS = 2
BF16 = jnp.bfloat16
F32 = jnp.float32


def leaf_perm(dz, dy):
    pairs = []
    for y in range(2):
        for z in range(8):
            pairs.append((y * 8 + z, (y ^ dy) * 8 + (z + dz) % 8))
    return pairs


def panel_perm(dx, dl, dc):
    pairs = []
    for x in range(4):
        for low in range(2):
            for core in range(2):
                target = ((x + dx) % 4) * 4 + (low ^ dl) * 2 + (core ^ dc)
                pairs.append((x * 4 + low * 2 + core, target))
    return pairs


def to_leaf(value, dz, dy=0):
    return lax.ppermute(value, "leaf", leaf_perm(dz, dy))


def to_panel(value, dx=0, dl=0, dc=0):
    return lax.ppermute(value, "panel", panel_perm(dx, dl, dc))


def destination(scalars, step, other):
    leaf = scalars[0]
    return ((leaf // 8) ^ other) * 8 + (leaf + step + 8) % 8


def window_slot(scalars, step, other):
    tile = destination(scalars, step, other)
    panel = scalars[1]
    ahead = (tile // 4 - panel // 4 + 4) % 4
    place = jnp.where(ahead == 0, 0, jnp.where(ahead == 3, 1, ahead + 1))
    return place * 2 + ((tile // 2) % 2 ^ (panel // 2) % 2)


def contribution_kernel(steps, sinks, scalars, factor, *refs):
    count = len(steps)
    trailing = refs[: 2 * count]
    own = refs[2 * count : 4 * count]
    across = refs[4 * count : 6 * count]
    outs = refs[6 * count :]
    core = scalars[1] % 2
    for at, step in enumerate(steps):
        pieces = []
        limits = []
        for other in range(2):
            tile = destination(scalars, step, other)
            mine = (tile % 2) == core
            pieces.append(jnp.where(mine, own[2 * at + other][0], across[2 * at + other][0]))
            limits.append(tile)
        weights = jnp.concatenate(pieces, axis=0)
        for k in range(TILES_DEV):
            child = scalars[2 + k]
            planned = scalars[10 + child]
            rows = pl.ds(pl.multiple_of(child * TILE, TILE), TILE)
            update = lax.dot_general(
                factor[rows, :], weights, (((1,), (1,)), ((), ())), preferred_element_type=F32
            )
            for other in range(2):
                part = update[:, other * TILE : (other + 1) * TILE]
                part = jnp.where(limits[other] < planned, part, 0.0)
                value = (trailing[2 * at + other][rows, :].astype(F32) - part).astype(BF16)
                sinks[(step, other)](outs, k, value)


def contributions(steps, out_shapes, sinks, scalars, factor, trailing, own, across):
    def column(step, other):
        return pl.BlockSpec((ROWS_DEV, TILE), lambda i, s: (0, destination(s, step, other)))

    def piece(step, other):
        return pl.BlockSpec((1, TILE, PW), lambda i, s: (window_slot(s, step, other), 0, 0))

    pairs = [(step, other) for step in steps for other in range(2)]

    def body(s, f, *refs):
        contribution_kernel(steps, sinks, s, f, *refs)

    return pl.pallas_call(
        body,
        out_shape=[jax.ShapeDtypeStruct(shape, BF16) for shape in out_shapes],
        grid_spec=pltpu.PrefetchScalarGridSpec(
            num_scalar_prefetch=1,
            grid=(1,),
            in_specs=[pl.BlockSpec((ROWS_DEV, PW), lambda i, s: (0, 0))]
            + [column(*pair) for pair in pairs]
            + [piece(*pair) for pair in pairs]
            + [piece(*pair) for pair in pairs],
            out_specs=[
                pl.BlockSpec(shape, lambda i, s, rank=len(shape): (0,) * rank) for shape in out_shapes
            ],
        ),
        compiler_params=pltpu.CompilerParams(vmem_limit_bytes=24 * 1024 * 1024),
        cost_estimate=pl.CostEstimate(
            flops=2 * ROWS_DEV * PW * 2 * TILE * len(steps),
            bytes_accessed=(1 + 2 * len(steps)) * ROWS_DEV * PW * 2,
            transcendentals=0,
        ),
    )(scalars, factor, *([trailing] * len(pairs)), *([own] * len(pairs)), *([across] * len(pairs)))


def into(slot, lead=None):
    def sink(outs, k, value):
        per = TILES_DEV // STREAMS
        group, inner = divmod(k, per)
        rows = pl.ds(inner * TILE, TILE)
        per_stream = len(outs) // STREAMS
        out = outs[group * per_stream + slot]
        if lead is None:
            out[rows, :] = value
        else:
            out[lead, rows, :] = value

    return sink


def add(*terms):
    total = terms[0].astype(F32)
    for term in terms[1:]:
        total = total + term.astype(F32)
    return total


def on_device(a21, l11_inv, a22, tasks, emap, parent_in):
    a21, l11_inv, a22 = a21[0], l11_inv[0], a22[0]

    def solve(rows):
        return lax.dot_general(
            rows, l11_inv, (((1,), (1,)), ((), ())), preferred_element_type=F32
        ).astype(BF16)

    lead = solve(a21[:TILE])
    pair = jnp.stack([lead, to_panel(lead, dl=1)])
    own = jnp.concatenate([pair, to_panel(pair, dx=1), to_panel(pair, dx=-1), to_panel(pair, dx=2)])
    across = to_panel(own, dc=1)

    factor = solve(a21)
    order = jnp.arange(TILES_DEV, dtype=jnp.int32)
    children = jnp.sum(jnp.where(emap[0][None, :] == order[:, None], order[None, :], 0), axis=1)
    scalars = jnp.concatenate(
        [
            lax.axis_index("leaf").astype(jnp.int32)[None],
            lax.axis_index("panel").astype(jnp.int32)[None],
            children.astype(jnp.int32),
            tasks[0],
        ]
    )
    rows = ROWS_DEV // STREAMS
    one, two, three = (rows, TILE), (2, rows, TILE), (3, rows, TILE)

    def run(steps, shapes, sinks):
        flat = contributions(steps, shapes * STREAMS, sinks, scalars, factor, a22, own, across)
        return [flat[g * len(shapes) : (g + 1) * len(shapes)] for g in range(STREAMS)]

    far = run([4], [one, one], {(4, 0): into(0), (4, 1): into(1)})
    up, down = [], []
    for g in range(STREAMS):
        up.append(to_leaf(far[g][0], 1))
        down.append(to_leaf(far[g][1], -1))
    third = run(
        [3, -3],
        [two, two],
        {(3, 0): into(0, 0), (3, 1): into(0, 1), (-3, 0): into(1, 0), (-3, 1): into(1, 1)},
    )
    near = run(
        [1, -1, 0],
        [one, one, one, three],
        {
            (1, 0): into(0),
            (-1, 0): into(1),
            (0, 0): into(2),
            (1, 1): into(3, 0),
            (-1, 1): into(3, 1),
            (0, 1): into(3, 2),
        },
    )
    direct = [to_leaf(near[g][3], 0, 1) for g in range(STREAMS)]
    second = run(
        [2, -2],
        [one, one, one, one],
        {(2, 0): into(0), (2, 1): into(1), (-2, 0): into(2), (-2, 1): into(3)},
    )
    for g in range(STREAMS):
        c3p, c3m = third[g]
        up[g] = to_leaf(jnp.stack([add(c3p[0], up[g]).astype(BF16), c3p[1]]), 1)
        down[g] = to_leaf(jnp.stack([c3m[0], add(c3m[1], down[g]).astype(BF16)]), -1)
    for g in range(STREAMS):
        c2ps, c2po, c2ms, c2mo = second[g]
        up[g] = (
            to_leaf(add(c2ps, up[g][0]).astype(BF16), 1),
            to_leaf(add(c2po, up[g][1]).astype(BF16), 1, 1),
        )
        down[g] = (
            to_leaf(add(c2ms, down[g][0]).astype(BF16), -1),
            to_leaf(add(c2mo, down[g][1]).astype(BF16), -1, 1),
        )
    total = []
    for g in range(STREAMS):
        c1p, c1m, c0, _ = near[g]
        up[g] = to_leaf(add(c1p, direct[g][0], *up[g]).astype(BF16), 1)
        down[g] = to_leaf(add(c1m, direct[g][1], *down[g]).astype(BF16), -1)
        total.append(add(c0, direct[g][2], up[g], down[g]))
    return (factor[None], parent_in + jnp.concatenate(total))


def solution(mesh):
    return jax.shard_map(
        on_device,
        mesh=mesh,
        in_specs=(
            P("leaf", "panel", None),
            P("leaf", None, None),
            P("leaf", "panel", None),
            P("leaf", "panel"),
            P("leaf", "panel"),
            P("panel", "leaf"),
        ),
        out_specs=(P("leaf", "panel", None), P("panel", "leaf")),
        check_vma=False,
    )
```

```python
import jax
import jax.numpy as jnp
from jax import lax
from jax.experimental import pallas as pl
from jax.experimental.pallas import tpu as pltpu
from jax.sharding import PartitionSpec as P

TILE = 128
TILES_DEV = 8
ROWS_DEV = TILES_DEV * TILE
PW = 256
BF16 = jnp.bfloat16
F32 = jnp.float32
AXES = ("leaf", "panel")
VMEM_LIMIT = 16 * 1024 * 1024


def place(value, move):
    pairs = []
    for y in range(2):
        for z in range(8):
            for x in range(4):
                for low in range(2):
                    for core in range(2):
                        ny, nz, nx, nlow, ncore = move(y, z, x, low, core)
                        target = ny * 8 + nz % 8, (nx % 4) * 4 + nlow * 2 + ncore
                        pairs.append(((y * 8 + z) * 16 + x * 4 + low * 2 + core, target[0] * 16 + target[1]))
    return lax.ppermute(value, AXES, pairs)


def to_sibling(value):
    return place(value, lambda y, z, x, low, core: (y, z, x, low, 1 - core))


def across_y(value):
    return place(value, lambda y, z, x, low, core: (1 - y, z, x, low, core))


def along(value):
    return place(value, lambda y, z, x, low, core: (y, z + 1 - 2 * core, x, low, core))


def along_crossing(value):
    return place(value, lambda y, z, x, low, core: (y, z + 1 - 2 * core, x, low, 1 - core))


def along_first(value):
    return place(value, lambda y, z, x, low, core: (y ^ core, z + 1 - 2 * core, x, low, core))


def along_second(value):
    return place(value, lambda y, z, x, low, core: (1 - (y ^ core), z + 1 - 2 * core, x, low, core))


def position():
    return lax.axis_index("leaf"), lax.axis_index("panel")


def destination(step, kind):
    leaf, panel = position()
    core = panel % 2
    other = {0: 0, 1: 1, 2: core, 3: 1 - core}[kind]
    z = leaf + step * (1 - 2 * core) + 8
    return ((leaf // 8) ^ other) * 8 + z % 8


def window_slot(step, kind):
    tile = destination(step, kind)
    panel = position()[1]
    ahead = (tile // 4 - panel // 4 + 4) % 4
    slot = jnp.where(ahead == 0, 0, jnp.where(ahead == 2, 1, jnp.where(ahead == 1, 2, 3)))
    return slot * 2 + ((tile // 2) % 2 ^ (panel // 2) % 2)


def contributions(items, out_shapes, maps, factors, trailings, window, inverse, after=None):
    tiles = []
    for _, step, kind, _, _ in items:
        if (step, kind) not in tiles:
            tiles.append((step, kind))
    panels = []
    for panel, *_ in items:
        if panel not in panels:
            panels.append(panel)
    groups = []
    for panel in panels:
        work = [item for item in items if item[0] == panel]
        groups += [(panel, work[first : first + 2]) for first in range(0, len(work), 2)]
    count = len(panels)

    def body(*refs):
        maps_ref = dict(zip(panels, refs[:count]))
        factor = dict(zip(panels, refs[count : 2 * count]))
        trailing = dict(zip(panels, refs[2 * count : 3 * count]))
        own, far, inverse_ref = refs[3 * count : 3 * count + 3]
        outs = refs[len(refs) - len(out_shapes) :]
        core = position()[1] % 2
        weights = {}
        for tile in tiles:
            mine = (destination(*tile) % 2) == core
            slot = window_slot(*tile)
            rows = jnp.where(mine, own[slot], far[slot])
            weights[tile] = lax.dot_general(
                rows, inverse_ref[...], (((1,), (1,)), ((), ())), preferred_element_type=F32
            ).astype(BF16)
        for panel, group in groups:
            weight = jnp.concatenate([weights[item[1:3]] for item in group], axis=0)
            for pair in range(TILES_DEV // 2):
                update = lax.dot_general(
                    factor[panel][pair * 2 * TILE : (pair + 1) * 2 * TILE, :], weight,
                    (((1,), (1,)), ((), ())), preferred_element_type=F32,
                )
                for t in (2 * pair, 2 * pair + 1):
                    rows = slice(t * TILE, (t + 1) * TILE)
                    inner = (t % 2) * TILE
                    target = pl.ds(pl.multiple_of(maps_ref[panel][0, t] * TILE, TILE), TILE)
                    for m, (_, step, kind, out, lead) in enumerate(group):
                        tile = destination(step, kind)
                        part = update[inner : inner + TILE, m * TILE : (m + 1) * TILE]
                        part = jnp.where(tile < maps_ref[panel][0, TILES_DEV + t], part, 0.0)
                        column = pl.ds(pl.multiple_of(tile * TILE, TILE), TILE)
                        value = (trailing[panel][rows, column].astype(F32) - part).astype(BF16)
                        outs[out][(*lead, target, slice(None))] = value

    here = pl.BlockSpec(memory_space=pltpu.VMEM)
    extra = [] if after is None else [after]
    return pl.pallas_call(
        body,
        out_shape=[jax.ShapeDtypeStruct(shape, BF16) for shape in out_shapes],
        in_specs=[pl.BlockSpec(memory_space=pltpu.SMEM)] * count + [here] * (2 * count + 3 + len(extra)),
        out_specs=[here] * len(out_shapes),
        compiler_params=pltpu.CompilerParams(vmem_limit_bytes=VMEM_LIMIT),
        cost_estimate=pl.CostEstimate(
            flops=2 * ROWS_DEV * PW * TILE * len(items),
            bytes_accessed=(count * PW + 2 * len(items) * TILE) * ROWS_DEV * 2,
            transcendentals=0,
        ),
    )(
        *[maps[panel] for panel in panels],
        *[factors[panel] for panel in panels],
        *[trailings[panel] for panel in panels],
        *window,
        inverse,
        *extra,
    )


def solve_kernel(a21, inverse, emap, tasks, out, kept):
    out[:ROWS_DEV, :] = lax.dot_general(
        a21[...], inverse[...], (((1,), (1,)), ((), ())), preferred_element_type=F32
    ).astype(BF16)
    kept[...] = inverse[...]
    row = lax.broadcasted_iota(jnp.int32, (2 * TILES_DEV, PW), 0)
    rows = jnp.zeros((2 * TILES_DEV, PW), F32)
    for t in range(TILES_DEV):
        rows = jnp.where(row == t, emap[0, t].astype(F32), rows)
        rows = jnp.where(row == TILES_DEV + t, tasks[0, t].astype(F32), rows)
    out[ROWS_DEV:, :] = rows.astype(BF16)


def solve(a21, inverse, emap, tasks):
    here = pl.BlockSpec(memory_space=pltpu.VMEM)
    scalars = pl.BlockSpec(memory_space=pltpu.SMEM)
    rows = (ROWS_DEV + 2 * TILES_DEV, PW)
    return pl.pallas_call(
        solve_kernel,
        out_shape=[jax.ShapeDtypeStruct(rows, BF16), jax.ShapeDtypeStruct(inverse.shape, BF16)],
        in_specs=[here] * 2 + [scalars] * 2,
        out_specs=[here] * 2,
        compiler_params=pltpu.CompilerParams(vmem_limit_bytes=VMEM_LIMIT),
        cost_estimate=pl.CostEstimate(
            flops=2 * ROWS_DEV * PW * PW, bytes_accessed=4 * ROWS_DEV * PW, transcendentals=0
        ),
    )(a21, inverse, emap, tasks)


def bring_kernel(trailing, pair, out):
    out[...] = trailing[:TILE, :TILE] + pair[0, :, :TILE]


def bring(trailing, pair):
    here = pl.BlockSpec(memory_space=pltpu.VMEM)
    return pl.pallas_call(
        bring_kernel,
        out_shape=jax.ShapeDtypeStruct((TILE, TILE), BF16),
        in_specs=[here] * 2,
        out_specs=here,
        compiler_params=pltpu.CompilerParams(vmem_limit_bytes=VMEM_LIMIT),
    )(trailing, pair)


def add(*terms):
    total = terms[0].astype(F32)
    for term in terms[1:]:
        total = total + term.astype(F32)
    return total


def on_device(a21, l11_inv, a22, tasks, emap, parent_in):
    a21, l11_inv, a22 = a21[0], l11_inv[0], a22[0]
    a22_other = to_sibling(a22)
    lead = a21[:TILE]
    pair = jnp.stack([lead, place(lead, lambda y, z, x, low, core: (y, z, x, 1 - low, core))])
    factor, inverse = solve(a21, l11_inv, emap, tasks)
    pair, factor, inverse = lax.optimization_barrier((pair, factor, inverse))
    factor_other = to_sibling(factor)
    own = jnp.concatenate(
        [pair]
        + [
            place(pair, lambda y, z, x, low, core, dx=dx: (y, z, x + dx, low, core))
            for dx in (2, -1, 1)
        ]
    )
    brought = bring(a22, pair)
    maps_other = factor_other[ROWS_DEV:, 0].astype(jnp.int32)[None]
    own, a22_other, factor_other, maps_other, brought = lax.optimization_barrier(
        (own, a22_other, factor_other, maps_other, brought)
    )
    window = (own, to_sibling(own))
    maps = (jnp.concatenate([emap, tasks], axis=1), maps_other)
    factors, trailings = (factor, factor_other), (a22, a22_other)

    def run(items, shapes, after=None):
        return contributions(items, shapes, maps, factors, trailings, window, inverse, after)

    one, two, three = (ROWS_DEV, TILE), (2, ROWS_DEV, TILE), (3, ROWS_DEV, TILE)
    (far,) = run([(0, 4, 2, 0, (0,)), (1, 4, 2, 0, (1,))], [two], brought)
    first = along(far)
    sib1, own1, own0, near = run(
        [
            (0, 1, 1, 3, (1,)), (0, 0, 1, 3, (2,)), (0, 1, 0, 1, ()), (0, 0, 0, 2, ()),
            (1, 1, 1, 3, (0,)), (1, 1, 0, 0, ()),
        ],
        [one, one, one, three],
        far,
    )
    beside = across_y(near)
    third = run(
        [(1, 3, 2, 0, (0,)), (1, 3, 3, 0, (1,)), (0, 3, 2, 1, (0,)), (0, 3, 3, 1, (1,))],
        [two, two],
        near,
    )
    second = run(
        [(1, 2, 2, 0, ()), (1, 2, 3, 1, ()), (0, 2, 2, 2, ()), (0, 2, 3, 3, ())],
        [one] * 4,
        third[0],
    )
    moving = []
    for g in range(2):
        moving.append(along(jnp.stack([add(third[g][0], first[1 - g]).astype(BF16), third[g][1]])))
    for g in range(2):
        if g == 0:
            moving[g], beside = lax.optimization_barrier((moving[g], beside))
        moving[g] = (
            along_first(add(second[2 * g], moving[g][0]).astype(BF16)),
            along_second(add(second[2 * g + 1], moving[g][1]).astype(BF16)),
        )
    for g, base in enumerate((sib1, own1)):
        total = add(base, beside[g], *moving[g]).astype(BF16)
        moving[g] = along(total) if g else along_crossing(total)
    arrivals = add(own0, beside[2], *moving)
    return (factor[None, :ROWS_DEV], parent_in + arrivals)


def solution(mesh):
    return jax.shard_map(
        on_device,
        mesh=mesh,
        in_specs=(
            P("leaf", "panel", None),
            P("leaf", None, None),
            P("leaf", "panel", None),
            P("leaf", "panel"),
            P("leaf", "panel"),
            P("panel", "leaf"),
        ),
        out_specs=(P("leaf", "panel", None), P("panel", "leaf")),
        check_vma=False,
    )
```

```python
import jax
import jax.numpy as jnp
from jax import lax
from jax.experimental import pallas as pl
from jax.experimental.pallas import tpu as pltpu
from jax.sharding import PartitionSpec as P

TILE = 128
TILES_DEV = 8
ROWS_DEV = TILES_DEV * TILE
PW = 256
BF16 = jnp.bfloat16
F32 = jnp.float32
AXES = ("leaf", "panel")
VMEM_LIMIT = 16 * 1024 * 1024


def place(value, move):
    pairs = []
    for y in range(2):
        for z in range(8):
            for x in range(4):
                for low in range(2):
                    for core in range(2):
                        ny, nz, nx, nlow, ncore = move(y, z, x, low, core)
                        target = ny * 8 + nz % 8, (nx % 4) * 4 + nlow * 2 + ncore
                        pairs.append(((y * 8 + z) * 16 + x * 4 + low * 2 + core, target[0] * 16 + target[1]))
    return lax.ppermute(value, AXES, pairs)


def to_sibling(value):
    return place(value, lambda y, z, x, low, core: (y, z, x, low, 1 - core))


def across_y(value):
    return place(value, lambda y, z, x, low, core: (1 - y, z, x, low, core))


def along(value, way):
    return place(value, lambda y, z, x, low, core: (y, z + way, x, low, core))


def along_y(value, way):
    return place(value, lambda y, z, x, low, core: (1 - y, z + way, x, low, core))


def position():
    return lax.axis_index("leaf"), lax.axis_index("panel")


def destination(step, other):
    leaf = position()[0]
    return ((leaf // 8) ^ other) * 8 + (leaf + step + 8) % 8


def window_slot(step, other):
    tile = destination(step, other)
    panel = position()[1]
    ahead = (tile // 4 - panel // 4 + 4) % 4
    slot = jnp.where(ahead == 0, 0, jnp.where(ahead == 2, 1, jnp.where(ahead == 1, 2, 3)))
    return slot * 2 + ((tile // 2) % 2 ^ (panel // 2) % 2)


def contributions(items, out_shapes, prepared, window, after):
    def body(factor, trailing, limits, inverse, own, far, after, *outs):
        core = position()[1] % 2
        for first in range(0, len(items), 2):
            group = items[first : first + 2]
            tiles = [destination(step, other) for step, other, _, _ in group]
            columns = [pl.ds(pl.multiple_of(tile * TILE, TILE), TILE) for tile in tiles]
            weights = []
            for tile, (step, other, _, _) in zip(tiles, group):
                mine = (tile % 2) == core
                slot = window_slot(step, other)
                rows = jnp.where(mine, own[slot], far[slot])
                weights.append(
                    lax.dot_general(
                        rows, inverse[...], (((1,), (1,)), ((), ())), preferred_element_type=F32
                    ).astype(BF16)
                )
            weight = jnp.concatenate(weights, axis=0)
            for pair in range(TILES_DEV // 2):
                update = lax.dot_general(
                    factor[pair * 2 * TILE : (pair + 1) * 2 * TILE, :], weight,
                    (((1,), (1,)), ((), ())), preferred_element_type=F32,
                )
                for k in (2 * pair, 2 * pair + 1):
                    rows = slice(k * TILE, (k + 1) * TILE)
                    inner = (k % 2) * TILE
                    for m, (_, _, out, lead) in enumerate(group):
                        part = update[inner : inner + TILE, m * TILE : (m + 1) * TILE]
                        part = jnp.where(limits[k : k + 1, :] > tiles[m], part, 0.0)
                        value = (trailing[rows, columns[m]].astype(F32) - part).astype(BF16)
                        outs[out][(*lead, rows, slice(None))] = value

    here = pl.BlockSpec(memory_space=pltpu.VMEM)
    return pl.pallas_call(
        body,
        out_shape=[jax.ShapeDtypeStruct(shape, BF16) for shape in out_shapes],
        in_specs=[here] * 7,
        out_specs=[here] * len(out_shapes),
        compiler_params=pltpu.CompilerParams(vmem_limit_bytes=VMEM_LIMIT),
        cost_estimate=pl.CostEstimate(
            flops=2 * ROWS_DEV * PW * TILE * len(items),
            bytes_accessed=(PW + 2 * len(items) * TILE) * ROWS_DEV * 2,
            transcendentals=0,
        ),
    )(*prepared, *window, after)


def prepare_kernel(maps, a21, inverse, trailing, out, factor, ordered, limits, kept):
    out[...] = lax.dot_general(
        a21[...], inverse[...], (((1,), (1,)), ((), ())), preferred_element_type=F32
    ).astype(BF16)
    kept[...] = inverse[...]
    for t in range(TILES_DEV):
        rows = slice(t * TILE, (t + 1) * TILE)
        target = pl.ds(pl.multiple_of(maps[0, t] * TILE, TILE), TILE)
        factor[target, :] = out[rows, :]
        ordered[target, :] = trailing[rows, :]
        limits[pl.ds(maps[0, t], 1), :] = jnp.full((1, TILE), maps[0, TILES_DEV + t], jnp.int32)


def prepare(maps, a21, inverse, trailing):
    here = pl.BlockSpec(memory_space=pltpu.VMEM)
    like = [jax.ShapeDtypeStruct(value.shape, BF16) for value in (a21, a21, trailing)]
    return pl.pallas_call(
        prepare_kernel,
        out_shape=like
        + [
            jax.ShapeDtypeStruct((TILES_DEV, TILE), jnp.int32),
            jax.ShapeDtypeStruct(inverse.shape, BF16),
        ],
        in_specs=[pl.BlockSpec(memory_space=pltpu.SMEM)] + [here] * 3,
        out_specs=[here] * 5,
        compiler_params=pltpu.CompilerParams(vmem_limit_bytes=VMEM_LIMIT),
        cost_estimate=pl.CostEstimate(
            flops=2 * ROWS_DEV * PW * PW, bytes_accessed=8 * 1024 * 1024, transcendentals=0
        ),
    )(maps, a21, inverse, trailing)


def bring_kernel(trailing, lead, out):
    out[...] = trailing[:TILE, :TILE] + lead[:, :TILE]


def bring(trailing, lead):
    here = pl.BlockSpec(memory_space=pltpu.VMEM)
    return pl.pallas_call(
        bring_kernel,
        out_shape=jax.ShapeDtypeStruct((TILE, TILE), BF16),
        in_specs=[here] * 2,
        out_specs=here,
        compiler_params=pltpu.CompilerParams(vmem_limit_bytes=VMEM_LIMIT),
    )(trailing, lead)


def add(*terms):
    total = terms[0].astype(F32)
    for term in terms[1:]:
        total = total + term.astype(F32)
    return total


def on_device(a21, l11_inv, a22, tasks, emap, parent_in):
    a21, l11_inv, a22 = a21[0], l11_inv[0], a22[0]
    lead = a21[:TILE]
    pair = jnp.stack([lead, place(lead, lambda y, z, x, low, core: (y, z, x, 1 - low, core))])
    pair, brought, a21, l11_inv = lax.optimization_barrier((pair, bring(a22, lead), a21, l11_inv))
    own = jnp.concatenate(
        [pair]
        + [
            place(pair, lambda y, z, x, low, core, dx=dx: (y, z, x + dx, low, core))
            for dx in (2, -1, 1)
        ]
    )
    maps = jnp.concatenate([emap, tasks], axis=1)
    l21, *prepared = prepare(maps, a21, l11_inv, a22)
    own, prepared = lax.optimization_barrier((own, prepared))
    window = (own, to_sibling(own))

    def run(items, shapes, after):
        return contributions(items, shapes, prepared, window, after)

    one, two = (ROWS_DEV, TILE), (2, ROWS_DEV, TILE)
    def bf16(*terms):
        return add(*terms).astype(BF16)

    far, far_y = run([(4, 0, 0, ()), (4, 1, 1, ())], [one, one], brought)
    up4, down4_y = along(far, 1), along(far_y, -1)
    near1, up3_y, down3 = run(
        [(3, 1, 1, ()), (-3, 0, 2, ()), (1, 1, 0, (0,)), (-1, 1, 0, (1,))], [two, one, one], far
    )
    up3, down3_y, near0 = run([(3, 0, 0, ()), (-3, 1, 1, ()), (0, 1, 2, ())], [one] * 3, up3_y)
    up3_y, down3 = along(up3_y, 1), along(down3, -1)
    near1 = across_y(near1)
    up = along(bf16(up3, up4), 1)
    down3_y = bf16(down3_y, down4_y)
    down_y = along(down3_y, -1)
    up2_y, down2, up2, down2_y = run(
        [(2, 1, 0, ()), (-2, 0, 1, ()), (2, 0, 2, ()), (-2, 1, 3, ())], [one] * 4, down3_y
    )
    up_y = along_y(bf16(up2_y, up3_y), 1)
    down = along(bf16(down2, down3), -1)
    up1, down1, own0 = run([(1, 0, 0, ()), (-1, 0, 1, ()), (0, 0, 2, ())], [one] * 3, up2)
    up = along(bf16(up2, up), 1)
    down_y = along_y(bf16(down2_y, down_y), -1)
    near1, near0 = lax.optimization_barrier((near1, near0))
    near0 = across_y(near0)
    up = along(bf16(up1, up, up_y, near1[0]), 1)
    down = along(bf16(down1, down, down_y, near1[1]), -1)
    arrivals = add(own0, near0, up, down)
    return (l21[None], parent_in + arrivals)


def solution(mesh):
    return jax.shard_map(
        on_device,
        mesh=mesh,
        in_specs=(
            P("leaf", "panel", None),
            P("leaf", None, None),
            P("leaf", "panel", None),
            P("leaf", "panel"),
            P("leaf", "panel"),
            P("panel", "leaf"),
        ),
        out_specs=(P("leaf", "panel", None), P("panel", "leaf")),
        check_vma=False,
    )
```

```python
import jax
import jax.numpy as jnp
from jax import lax
from jax.experimental import pallas as pl
from jax.experimental.pallas import tpu as pltpu
from jax.sharding import PartitionSpec as P

TILE = 128
TILES_DEV = 8
ROWS_DEV = TILES_DEV * TILE
PW = 256
BF16 = jnp.bfloat16
F32 = jnp.float32
AXES = ("leaf", "panel")
VMEM_LIMIT = 16 * 1024 * 1024


def place(value, move):
    pairs = []
    for y in range(2):
        for z in range(8):
            for x in range(4):
                for low in range(2):
                    for core in range(2):
                        ny, nz, nx, nlow, ncore = move(y, z, x, low, core)
                        target = ny * 8 + nz % 8, (nx % 4) * 4 + nlow * 2 + ncore
                        pairs.append(((y * 8 + z) * 16 + x * 4 + low * 2 + core, target[0] * 16 + target[1]))
    return lax.ppermute(value, AXES, pairs)


def to_sibling(value):
    return place(value, lambda y, z, x, low, core: (y, z, x, low, 1 - core))


def across_y(value):
    return place(value, lambda y, z, x, low, core: (1 - y, z, x, low, core))


def along(value, way):
    return place(value, lambda y, z, x, low, core: (y, z + way, x, low, core))


def along_y(value, way):
    return place(value, lambda y, z, x, low, core: (1 - y, z + way, x, low, core))


def position():
    return lax.axis_index("leaf"), lax.axis_index("panel")


def destination(step, other):
    leaf = position()[0]
    return ((leaf // 8) ^ other) * 8 + (leaf + step + 8) % 8


def window_slot(step, other):
    tile = destination(step, other)
    panel = position()[1]
    ahead = (tile // 4 - panel // 4 + 4) % 4
    slot = jnp.where(ahead == 0, 0, jnp.where(ahead == 2, 1, jnp.where(ahead == 1, 2, 3)))
    return slot * 2 + ((tile // 2) % 2 ^ (panel // 2) % 2)


def contributions(items, out_shapes, prepared, window, after):
    def body(factor, trailing, limits, inverse, own, far, after, *outs):
        core = position()[1] % 2
        for first in range(0, len(items), 2):
            group = items[first : first + 2]
            tiles = [destination(step, other) for step, other, _, _ in group]
            columns = [pl.ds(pl.multiple_of(tile * TILE, TILE), TILE) for tile in tiles]
            weights = []
            for tile, (step, other, _, _) in zip(tiles, group):
                mine = (tile % 2) == core
                slot = window_slot(step, other)
                rows = jnp.where(mine, own[slot], far[slot])
                weights.append(
                    lax.dot_general(
                        rows, inverse[...], (((1,), (1,)), ((), ())), preferred_element_type=F32
                    ).astype(BF16)
                )
            weight = jnp.concatenate(weights, axis=0)
            for pair in range(TILES_DEV // 2):
                update = lax.dot_general(
                    factor[pair * 2 * TILE : (pair + 1) * 2 * TILE, :], weight,
                    (((1,), (1,)), ((), ())), preferred_element_type=F32,
                )
                for k in (2 * pair, 2 * pair + 1):
                    rows = slice(k * TILE, (k + 1) * TILE)
                    inner = (k % 2) * TILE
                    for m, (_, _, out, lead) in enumerate(group):
                        part = update[inner : inner + TILE, m * TILE : (m + 1) * TILE]
                        part = jnp.where(limits[k : k + 1, :] > tiles[m], part, 0.0)
                        value = (trailing[rows, columns[m]].astype(F32) - part).astype(BF16)
                        outs[out][(*lead, rows, slice(None))] = value

    here = pl.BlockSpec(memory_space=pltpu.VMEM)
    return pl.pallas_call(
        body,
        out_shape=[jax.ShapeDtypeStruct(shape, BF16) for shape in out_shapes],
        in_specs=[here] * 7,
        out_specs=[here] * len(out_shapes),
        compiler_params=pltpu.CompilerParams(vmem_limit_bytes=VMEM_LIMIT),
        cost_estimate=pl.CostEstimate(
            flops=2 * ROWS_DEV * PW * TILE * len(items),
            bytes_accessed=(PW + 2 * len(items) * TILE) * ROWS_DEV * 2,
            transcendentals=0,
        ),
    )(*prepared, *window, after)


def prepare_kernel(maps, a21, inverse, trailing, out, factor, ordered, limits, kept):
    out[...] = lax.dot_general(
        a21[...], inverse[...], (((1,), (1,)), ((), ())), preferred_element_type=F32
    ).astype(BF16)
    kept[...] = inverse[...]
    for t in range(TILES_DEV):
        rows = slice(t * TILE, (t + 1) * TILE)
        target = pl.ds(pl.multiple_of(maps[0, t] * TILE, TILE), TILE)
        factor[target, :] = out[rows, :]
        ordered[target, :] = trailing[rows, :]
        limits[pl.ds(maps[0, t], 1), :] = jnp.full((1, TILE), maps[0, TILES_DEV + t], jnp.int32)


def prepare(maps, a21, inverse, trailing):
    here = pl.BlockSpec(memory_space=pltpu.VMEM)
    like = [jax.ShapeDtypeStruct(value.shape, BF16) for value in (a21, a21, trailing)]
    return pl.pallas_call(
        prepare_kernel,
        out_shape=like
        + [
            jax.ShapeDtypeStruct((TILES_DEV, TILE), jnp.int32),
            jax.ShapeDtypeStruct(inverse.shape, BF16),
        ],
        in_specs=[pl.BlockSpec(memory_space=pltpu.SMEM)] + [here] * 3,
        out_specs=[here] * 5,
        compiler_params=pltpu.CompilerParams(vmem_limit_bytes=VMEM_LIMIT),
        cost_estimate=pl.CostEstimate(
            flops=2 * ROWS_DEV * PW * PW, bytes_accessed=8 * 1024 * 1024, transcendentals=0
        ),
    )(maps, a21, inverse, trailing)


def bring_kernel(trailing, lead, out):
    out[...] = trailing[:TILE, :TILE] + lead[:, :TILE]


def bring(trailing, lead):
    here = pl.BlockSpec(memory_space=pltpu.VMEM)
    return pl.pallas_call(
        bring_kernel,
        out_shape=jax.ShapeDtypeStruct((TILE, TILE), BF16),
        in_specs=[here] * 2,
        out_specs=here,
        compiler_params=pltpu.CompilerParams(vmem_limit_bytes=VMEM_LIMIT),
    )(trailing, lead)


def add(*terms):
    total = terms[0].astype(F32)
    for term in terms[1:]:
        total = total + term.astype(F32)
    return total


def on_device(a21, l11_inv, a22, tasks, emap, parent_in):
    a21, l11_inv, a22 = a21[0], l11_inv[0], a22[0]
    lead = a21[:TILE]
    pair = jnp.stack([lead, place(lead, lambda y, z, x, low, core: (y, z, x, 1 - low, core))])
    pair, brought, a21, l11_inv = lax.optimization_barrier((pair, bring(a22, lead), a21, l11_inv))
    own = jnp.concatenate(
        [pair]
        + [
            place(pair, lambda y, z, x, low, core, dx=dx: (y, z, x + dx, low, core))
            for dx in (2, -1, 1)
        ]
    )
    maps = jnp.concatenate([emap, tasks], axis=1)
    l21, *prepared = prepare(maps, a21, l11_inv, a22)
    own, prepared = lax.optimization_barrier((own, prepared))
    window = (own, to_sibling(own))

    def run(items, shapes, after):
        return contributions(items, shapes, prepared, window, after)

    one, two = (ROWS_DEV, TILE), (2, ROWS_DEV, TILE)
    def bf16(*terms):
        return add(*terms).astype(BF16)

    far, far_y = run([(4, 0, 0, ()), (4, 1, 1, ())], [one, one], brought)
    up4, down4_y = along(far, 1), along(far_y, -1)
    next_y, next_ = run([(3, 1, 0, ()), (-3, 0, 1, ())], [one, one], far)
    up3_y, down3 = along(next_y, 1), along(next_, -1)
    near1, near0, up3, down3_y = run(
        [(1, 1, 0, (0,)), (-1, 1, 0, (1,)), (3, 0, 2, ()), (-3, 1, 3, ()), (0, 1, 1, ())],
        [two, one, one, one],
        next_y,
    )
    near1 = across_y(near1)
    up = along(bf16(up3, up4), 1)
    down3_y = bf16(down3_y, down4_y)
    down_y = along(down3_y, -1)
    up2_y, down2, up2, down2_y = run(
        [(2, 1, 0, ()), (-2, 0, 1, ()), (2, 0, 2, ()), (-2, 1, 3, ())], [one] * 4, down3_y
    )
    up_y = along_y(bf16(up2_y, up3_y), 1)
    down = along(bf16(down2, down3), -1)
    up1, down1, own0 = run([(1, 0, 0, ()), (-1, 0, 1, ()), (0, 0, 2, ())], [one] * 3, up2)
    up = along(bf16(up2, up), 1)
    down_y = along_y(bf16(down2_y, down_y), -1)
    up_y, near0 = lax.optimization_barrier((up_y, near0))
    near0 = across_y(near0)
    up, down1 = lax.optimization_barrier((bf16(up1, up, up_y, near1[0]), down1))
    up = along(up, 1)
    down = along(bf16(down1, down, down_y, near1[1]), -1)
    arrivals = add(own0, near0, up, down)
    return (l21[None], parent_in + arrivals)


def solution(mesh):
    return jax.shard_map(
        on_device,
        mesh=mesh,
        in_specs=(
            P("leaf", "panel", None),
            P("leaf", None, None),
            P("leaf", "panel", None),
            P("leaf", "panel"),
            P("leaf", "panel"),
            P("panel", "leaf"),
        ),
        out_specs=(P("leaf", "panel", None), P("panel", "leaf")),
        check_vma=False,
    )
```

```python
import jax
import jax.numpy as jnp
from jax import lax
from jax.experimental import pallas as pl
from jax.experimental.pallas import tpu as pltpu
from jax.sharding import PartitionSpec as P

TILE = 128
TILES_DEV = 8
ROWS_DEV = TILES_DEV * TILE
PW = 256
BF16 = jnp.bfloat16
F32 = jnp.float32
AXES = ("leaf", "panel")
VMEM_LIMIT = 16 * 1024 * 1024


def place(value, move):
    pairs = []
    for y in range(2):
        for z in range(8):
            for x in range(4):
                for low in range(2):
                    for core in range(2):
                        ny, nz, nx, nlow, ncore = move(y, z, x, low, core)
                        target = ny * 8 + nz % 8, (nx % 4) * 4 + nlow * 2 + ncore
                        pairs.append(((y * 8 + z) * 16 + x * 4 + low * 2 + core, target[0] * 16 + target[1]))
    return lax.ppermute(value, AXES, pairs)


def to_sibling(value):
    return place(value, lambda y, z, x, low, core: (y, z, x, low, 1 - core))


def across_y(value):
    return place(value, lambda y, z, x, low, core: (1 - y, z, x, low, core))


def along(value, way):
    return place(value, lambda y, z, x, low, core: (y, z + way, x, low, core))


def along_y(value, way):
    return place(value, lambda y, z, x, low, core: (1 - y, z + way, x, low, core))


def position():
    return lax.axis_index("leaf"), lax.axis_index("panel")


def destination(step, other):
    leaf = position()[0]
    return ((leaf // 8) ^ other) * 8 + (leaf + step + 8) % 8


def window_piece(tile, head, rest, far):
    panel = position()[1]
    core = panel % 2
    ahead = (tile // 4 - panel // 4 + 4) % 4
    low = (tile // 2) % 2 ^ (panel // 2) % 2
    mine = (tile % 2) == core
    holder = jnp.where(ahead == 0, tile % 2, jnp.where(ahead == 1, 1 - low, low))
    first = jnp.where(ahead == 2, 3, 1 + 4 * low)
    place_in = jnp.where(ahead == 0, 0, first + jnp.where(tile % 2 == holder, 0, 1))
    received = jnp.where(holder == core, rest[place_in], far[place_in])
    return jnp.where((ahead == 0) & (low == 0), head[jnp.where(mine, 0, 1)], received)


def gather_window(lead, head):
    beside = place(lead, lambda y, z, x, low, core: (y, z, x, 1 - low, core))
    sides = place(head, lambda y, z, x, low, core: (y, z, x + 1 - 2 * core, low, core))
    opposite = place(head, lambda y, z, x, low, core: (y, z, x + 2, low ^ core, core))
    corners = place(head, lambda y, z, x, low, core: (y, z, x - 1 + 2 * core, 1 - low, core))
    return jnp.concatenate([beside[None], sides, opposite, corners])


def contributions(items, out_shapes, prepared, window, after):
    def body(factor, trailing, limits, inverse, head, rest, far, after, *outs):
        for first in range(0, len(items), 2):
            group = items[first : first + 2]
            tiles = [destination(step, other) for step, other, _, _ in group]
            columns = [pl.ds(pl.multiple_of(tile * TILE, TILE), TILE) for tile in tiles]
            weights = []
            for tile in tiles:
                rows = window_piece(tile, head, rest, far)
                weights.append(
                    lax.dot_general(
                        rows, inverse[...], (((1,), (1,)), ((), ())), preferred_element_type=F32
                    ).astype(BF16)
                )
            weight = jnp.concatenate(weights, axis=0)
            for pair in range(TILES_DEV // 2):
                update = lax.dot_general(
                    factor[pair * 2 * TILE : (pair + 1) * 2 * TILE, :], weight,
                    (((1,), (1,)), ((), ())), preferred_element_type=F32,
                )
                for k in (2 * pair, 2 * pair + 1):
                    rows = slice(k * TILE, (k + 1) * TILE)
                    inner = (k % 2) * TILE
                    for m, (_, _, out, lead) in enumerate(group):
                        part = update[inner : inner + TILE, m * TILE : (m + 1) * TILE]
                        part = jnp.where(limits[k : k + 1, :] > tiles[m], part, 0.0)
                        value = (trailing[rows, columns[m]].astype(F32) - part).astype(BF16)
                        outs[out][(*lead, rows, slice(None))] = value

    here = pl.BlockSpec(memory_space=pltpu.VMEM)
    return pl.pallas_call(
        body,
        out_shape=[jax.ShapeDtypeStruct(shape, BF16) for shape in out_shapes],
        in_specs=[here] * 8,
        out_specs=[here] * len(out_shapes),
        compiler_params=pltpu.CompilerParams(vmem_limit_bytes=VMEM_LIMIT),
        cost_estimate=pl.CostEstimate(
            flops=2 * ROWS_DEV * PW * TILE * len(items),
            bytes_accessed=(PW + 2 * len(items) * TILE) * ROWS_DEV * 2,
            transcendentals=0,
        ),
    )(*prepared, *window, after)


def order_kernel(maps, trailing, ordered, limits):
    for t in range(TILES_DEV):
        target = pl.ds(pl.multiple_of(maps[0, t] * TILE, TILE), TILE)
        ordered[target, :] = trailing[t * TILE : (t + 1) * TILE, :]
        limits[pl.ds(maps[0, t], 1), :] = jnp.full((1, TILE), maps[0, TILES_DEV + t], jnp.int32)


def solve_kernel(maps, a21, inverse, out, factor, kept):
    out[...] = lax.dot_general(
        a21[...], inverse[...], (((1,), (1,)), ((), ())), preferred_element_type=F32
    ).astype(BF16)
    kept[...] = inverse[...]
    for t in range(TILES_DEV):
        target = pl.ds(pl.multiple_of(maps[0, t] * TILE, TILE), TILE)
        factor[target, :] = out[t * TILE : (t + 1) * TILE, :]


def in_vmem(kernel, flops, out_shape, maps, *operands):
    here = pl.BlockSpec(memory_space=pltpu.VMEM)
    return pl.pallas_call(
        kernel,
        out_shape=out_shape,
        in_specs=[pl.BlockSpec(memory_space=pltpu.SMEM)] + [here] * len(operands),
        out_specs=[here] * len(out_shape),
        compiler_params=pltpu.CompilerParams(vmem_limit_bytes=VMEM_LIMIT),
        cost_estimate=pl.CostEstimate(
            flops=flops, bytes_accessed=4 * 1024 * 1024, transcendentals=0
        ),
    )(maps, *operands)


def order(maps, trailing):
    shapes = [
        jax.ShapeDtypeStruct(trailing.shape, BF16),
        jax.ShapeDtypeStruct((TILES_DEV, TILE), jnp.int32),
    ]
    return in_vmem(order_kernel, 0, shapes, maps, trailing)


def solve(maps, a21, inverse):
    shapes = [jax.ShapeDtypeStruct(value.shape, BF16) for value in (a21, a21, inverse)]
    return in_vmem(solve_kernel, 2 * ROWS_DEV * PW * PW, shapes, maps, a21, inverse)


def add(*terms):
    total = terms[0].astype(F32)
    for term in terms[1:]:
        total = total + term.astype(F32)
    return total


def on_device(a21, l11_inv, a22, tasks, emap, parent_in):
    a21, l11_inv, a22 = a21[0], l11_inv[0], a22[0]
    lead = a21[:TILE]
    maps = jnp.concatenate([emap, tasks], axis=1)
    head, maps, a22 = lax.optimization_barrier((jnp.stack([lead, to_sibling(lead)]), maps, a22))
    rest = gather_window(lead, head)
    ordered, limits = order(maps, a22)
    rest, ordered, a21, l11_inv = lax.optimization_barrier((rest, ordered, a21, l11_inv))
    l21, factor, inverse = solve(maps, a21, l11_inv)
    prepared = factor, ordered, limits, inverse
    window = (head, rest, to_sibling(rest))

    def run(items, shapes, after):
        return contributions(items, shapes, prepared, window, after)

    one, two = (ROWS_DEV, TILE), (2, ROWS_DEV, TILE)
    def bf16(*terms):
        return add(*terms).astype(BF16)

    far, far_y = run([(4, 0, 0, ()), (4, 1, 1, ())], [one, one], prepared[0])
    up4, down4_y = along(far, 1), along(far_y, -1)
    next_y, next_ = run([(3, 1, 0, ()), (-3, 0, 1, ())], [one, one], far)
    up3_y, down3 = along(next_y, 1), along(next_, -1)
    near1, near0, up3, down3_y = run(
        [(1, 1, 0, (0,)), (-1, 1, 0, (1,)), (3, 0, 2, ()), (-3, 1, 3, ()), (0, 1, 1, ())],
        [two, one, one, one],
        next_y,
    )
    near1 = across_y(near1)
    up = along(bf16(up3, up4), 1)
    down3_y = bf16(down3_y, down4_y)
    down_y = along(down3_y, -1)
    up2_y, down2, up2, down2_y = run(
        [(2, 1, 0, ()), (-2, 0, 1, ()), (2, 0, 2, ()), (-2, 1, 3, ())], [one] * 4, down3_y
    )
    up_y = along_y(bf16(up2_y, up3_y), 1)
    down = along(bf16(down2, down3), -1)
    up1, down1, own0 = run([(1, 0, 0, ()), (-1, 0, 1, ()), (0, 0, 2, ())], [one] * 3, up2)
    up = along(bf16(up2, up), 1)
    down_y = along_y(bf16(down2_y, down_y), -1)
    up_y, near0 = lax.optimization_barrier((up_y, near0))
    near0 = across_y(near0)
    up, down1 = lax.optimization_barrier((bf16(up1, up, up_y, near1[0]), down1))
    up = along(up, 1)
    down = along(bf16(down1, down, down_y, near1[1]), -1)
    arrivals = add(own0, near0, up, down)
    return (l21[None], parent_in + arrivals)


def solution(mesh):
    return jax.shard_map(
        on_device,
        mesh=mesh,
        in_specs=(
            P("leaf", "panel", None),
            P("leaf", None, None),
            P("leaf", "panel", None),
            P("leaf", "panel"),
            P("leaf", "panel"),
            P("panel", "leaf"),
        ),
        out_specs=(P("leaf", "panel", None), P("panel", "leaf")),
        check_vma=False,
    )
```

```python
import jax
import jax.numpy as jnp
from jax import lax
from jax.experimental import pallas as pl
from jax.experimental.pallas import tpu as pltpu
from jax.sharding import PartitionSpec as P

TILE = 128
TILES_DEV = 8
ROWS_DEV = TILES_DEV * TILE
PW = 256
BF16 = jnp.bfloat16
F32 = jnp.float32
AXES = ("leaf", "panel")
VMEM_LIMIT = 16 * 1024 * 1024


def place(value, move):
    pairs = []
    for y in range(2):
        for z in range(8):
            for x in range(4):
                for low in range(2):
                    for core in range(2):
                        ny, nz, nx, nlow, ncore = move(y, z, x, low, core)
                        target = ny * 8 + nz % 8, (nx % 4) * 4 + nlow * 2 + ncore
                        pairs.append(((y * 8 + z) * 16 + x * 4 + low * 2 + core, target[0] * 16 + target[1]))
    return lax.ppermute(value, AXES, pairs)


def to_sibling(value):
    return place(value, lambda y, z, x, low, core: (y, z, x, low, 1 - core))


def across_y(value):
    return place(value, lambda y, z, x, low, core: (1 - y, z, x, low, core))


def along(value, way):
    return place(value, lambda y, z, x, low, core: (y, z + way, x, low, core))


def along_y(value, way):
    return place(value, lambda y, z, x, low, core: (1 - y, z + way, x, low, core))


def position():
    return lax.axis_index("leaf"), lax.axis_index("panel")


def destination(step, other):
    leaf = position()[0]
    return ((leaf // 8) ^ other) * 8 + (leaf + step + 8) % 8


def window_piece(tile, head, rest, far):
    panel = position()[1]
    core = panel % 2
    ahead = (tile // 4 - panel // 4 + 4) % 4
    low = (tile // 2) % 2 ^ (panel // 2) % 2
    mine = (tile % 2) == core
    holder = jnp.where(ahead == 0, tile % 2, jnp.where(ahead == 1, 1 - low, low))
    first = jnp.where(ahead == 2, 3, 1 + 4 * low)
    place_in = jnp.where(ahead == 0, 0, first + jnp.where(tile % 2 == holder, 0, 1))
    received = jnp.where(holder == core, rest[place_in], far[place_in])
    return jnp.where((ahead == 0) & (low == 0), head[jnp.where(mine, 0, 1)], received)


def gather_window(lead, head):
    beside = place(lead, lambda y, z, x, low, core: (y, z, x, 1 - low, core))
    sides = place(head, lambda y, z, x, low, core: (y, z, x + 1 - 2 * core, low, core))
    opposite = place(head, lambda y, z, x, low, core: (y, z, x + 2, low ^ core, core))
    corners = place(head, lambda y, z, x, low, core: (y, z, x - 1 + 2 * core, 1 - low, core))
    return jnp.concatenate([beside[None], sides, opposite, corners])


def contributions(items, out_shapes, prepared, window, after):
    def body(factor, trailing, limits, inverse, head, rest, far, after, *outs):
        for first in range(0, len(items), 2):
            group = items[first : first + 2]
            tiles = [destination(step, other) for step, other, _, _ in group]
            columns = [pl.ds(pl.multiple_of(tile * TILE, TILE), TILE) for tile in tiles]
            weights = []
            for tile in tiles:
                rows = window_piece(tile, head, rest, far)
                weights.append(
                    lax.dot_general(
                        rows, inverse[...], (((1,), (1,)), ((), ())), preferred_element_type=F32
                    ).astype(BF16)
                )
            weight = jnp.concatenate(weights, axis=0)
            for pair in range(TILES_DEV // 2):
                update = lax.dot_general(
                    factor[pair * 2 * TILE : (pair + 1) * 2 * TILE, :], weight,
                    (((1,), (1,)), ((), ())), preferred_element_type=F32,
                )
                for k in (2 * pair, 2 * pair + 1):
                    rows = slice(k * TILE, (k + 1) * TILE)
                    inner = (k % 2) * TILE
                    for m, (_, _, out, lead) in enumerate(group):
                        part = update[inner : inner + TILE, m * TILE : (m + 1) * TILE]
                        part = jnp.where(limits[k : k + 1, :] > tiles[m], part, 0.0)
                        value = (trailing[rows, columns[m]].astype(F32) - part).astype(BF16)
                        outs[out][(*lead, rows, slice(None))] = value

    here = pl.BlockSpec(memory_space=pltpu.VMEM)
    return pl.pallas_call(
        body,
        out_shape=[jax.ShapeDtypeStruct(shape, BF16) for shape in out_shapes],
        in_specs=[here] * 8,
        out_specs=[here] * len(out_shapes),
        compiler_params=pltpu.CompilerParams(vmem_limit_bytes=VMEM_LIMIT),
        cost_estimate=pl.CostEstimate(
            flops=2 * ROWS_DEV * PW * TILE * len(items),
            bytes_accessed=(PW + 2 * len(items) * TILE) * ROWS_DEV * 2,
            transcendentals=0,
        ),
    )(*prepared, *window, after)


def order_kernel(maps, trailing, ordered, limits):
    for t in range(TILES_DEV):
        target = pl.ds(pl.multiple_of(maps[0, t] * TILE, TILE), TILE)
        ordered[target, :] = trailing[t * TILE : (t + 1) * TILE, :]
        limits[pl.ds(maps[0, t], 1), :] = jnp.full((1, TILE), maps[0, TILES_DEV + t], jnp.int32)


def solve_kernel(maps, a21, inverse, out, factor, kept):
    out[...] = lax.dot_general(
        a21[...], inverse[...], (((1,), (1,)), ((), ())), preferred_element_type=F32
    ).astype(BF16)
    kept[...] = inverse[...]
    for t in range(TILES_DEV):
        target = pl.ds(pl.multiple_of(maps[0, t] * TILE, TILE), TILE)
        factor[target, :] = out[t * TILE : (t + 1) * TILE, :]


def in_vmem(kernel, flops, out_shape, maps, *operands):
    here = pl.BlockSpec(memory_space=pltpu.VMEM)
    return pl.pallas_call(
        kernel,
        out_shape=out_shape,
        in_specs=[pl.BlockSpec(memory_space=pltpu.SMEM)] + [here] * len(operands),
        out_specs=[here] * len(out_shape),
        compiler_params=pltpu.CompilerParams(vmem_limit_bytes=VMEM_LIMIT),
        cost_estimate=pl.CostEstimate(
            flops=flops, bytes_accessed=4 * 1024 * 1024, transcendentals=0
        ),
    )(maps, *operands)


def order(maps, trailing):
    shapes = [
        jax.ShapeDtypeStruct(trailing.shape, BF16),
        jax.ShapeDtypeStruct((TILES_DEV, TILE), jnp.int32),
    ]
    return in_vmem(order_kernel, 0, shapes, maps, trailing)


def solve(maps, a21, inverse):
    shapes = [jax.ShapeDtypeStruct(value.shape, BF16) for value in (a21, a21, inverse)]
    return in_vmem(solve_kernel, 2 * ROWS_DEV * PW * PW, shapes, maps, a21, inverse)


def add(*terms):
    total = terms[0].astype(F32)
    for term in terms[1:]:
        total = total + term.astype(F32)
    return total


def on_device(a21, l11_inv, a22, tasks, emap, parent_in):
    a21, l11_inv, a22 = a21[0], l11_inv[0], a22[0]
    lead = a21[:TILE]
    maps = jnp.concatenate([emap, tasks], axis=1)
    head, maps, a22 = lax.optimization_barrier((jnp.stack([lead, to_sibling(lead)]), maps, a22))
    rest = gather_window(lead, head)
    ordered, limits = order(maps, a22)
    rest, ordered, a21, l11_inv = lax.optimization_barrier((rest, ordered, a21, l11_inv))
    l21, factor, inverse = solve(maps, a21, l11_inv)
    prepared = factor, ordered, limits, inverse
    window = (head, rest, to_sibling(rest))

    def run(items, shapes, after):
        return contributions(items, shapes, prepared, window, after)

    one, two = (ROWS_DEV, TILE), (2, ROWS_DEV, TILE)
    def bf16(*terms):
        return add(*terms).astype(BF16)

    far, far_y = run([(4, 0, 0, ()), (4, 1, 1, ())], [one, one], prepared[0])
    up4, down4_y = along(far, 1), along(far_y, -1)
    next_y, next_ = run([(3, 1, 0, ()), (-3, 0, 1, ())], [one, one], far)
    up3_y, down3 = along(next_y, 1), along(next_, -1)
    near1, near0, up3, down3_y = run(
        [(1, 1, 0, (0,)), (-1, 1, 0, (1,)), (3, 0, 2, ()), (-3, 1, 3, ()), (0, 1, 1, ())],
        [two, one, one, one],
        next_y,
    )
    near1 = across_y(near1)
    up = along(bf16(up3, up4), 1)
    down3_y = bf16(down3_y, down4_y)
    down_y = along(down3_y, -1)
    up2_y, down2, up2, down2_y = run(
        [(2, 1, 0, ()), (-2, 0, 1, ()), (2, 0, 2, ()), (-2, 1, 3, ())], [one] * 4, down3_y
    )
    up_y = along_y(bf16(up2_y, up3_y), 1)
    down = along(bf16(down2, down3), -1)
    up1, own0 = run([(1, 0, 0, ()), (0, 0, 1, ())], [one] * 2, up2)
    up = along(bf16(up2, up), 1)
    down_y = along_y(bf16(down2_y, down_y), -1)
    up_y, near0 = lax.optimization_barrier((up_y, near0))
    near0 = across_y(near0)
    up = along(bf16(up1, up, up_y, near1[0]), 1)
    (down1,) = run([(-1, 0, 0, ())], [one], down_y)
    down = along(bf16(down1, down, down_y, near1[1]), -1)
    arrivals = add(own0, near0, up, down)
    return (l21[None], parent_in + arrivals)


def solution(mesh):
    return jax.shard_map(
        on_device,
        mesh=mesh,
        in_specs=(
            P("leaf", "panel", None),
            P("leaf", None, None),
            P("leaf", "panel", None),
            P("leaf", "panel"),
            P("leaf", "panel"),
            P("panel", "leaf"),
        ),
        out_specs=(P("leaf", "panel", None), P("panel", "leaf")),
        check_vma=False,
    )
```

```python
import jax
import jax.numpy as jnp
from jax import lax
from jax.experimental import pallas as pl
from jax.experimental.pallas import tpu as pltpu
from jax.sharding import PartitionSpec as P

TILE = 128
TILES_DEV = 8
ROWS_DEV = TILES_DEV * TILE
PW = 256
BF16 = jnp.bfloat16
F32 = jnp.float32
AXES = ("leaf", "panel")
VMEM_LIMIT = 16 * 1024 * 1024


def place(value, move):
    pairs = []
    for y in range(2):
        for z in range(8):
            for x in range(4):
                for low in range(2):
                    for core in range(2):
                        ny, nz, nx, nlow, ncore = move(y, z, x, low, core)
                        target = ny * 8 + nz % 8, (nx % 4) * 4 + nlow * 2 + ncore
                        pairs.append(((y * 8 + z) * 16 + x * 4 + low * 2 + core, target[0] * 16 + target[1]))
    return lax.ppermute(value, AXES, pairs)


def to_sibling(value):
    return place(value, lambda y, z, x, low, core: (y, z, x, low, 1 - core))


def across_y(value):
    return place(value, lambda y, z, x, low, core: (1 - y, z, x, low, core))


def along(value, way):
    return place(value, lambda y, z, x, low, core: (y, z + way, x, low, core))


def along_y(value, way):
    return place(value, lambda y, z, x, low, core: (1 - y, z + way, x, low, core))


def position():
    return lax.axis_index("leaf"), lax.axis_index("panel")


def destination(step, other):
    leaf = position()[0]
    return ((leaf // 8) ^ other) * 8 + (leaf + step + 8) % 8


def window_piece(tile, head, rest, far):
    panel = position()[1]
    core = panel % 2
    ahead = (tile // 4 - panel // 4 + 4) % 4
    low = (tile // 2) % 2 ^ (panel // 2) % 2
    mine = (tile % 2) == core
    holder = jnp.where(ahead == 0, tile % 2, jnp.where(ahead == 1, 1 - low, low))
    first = jnp.where(ahead == 2, 3, 1 + 4 * low)
    place_in = jnp.where(ahead == 0, 0, first + jnp.where(tile % 2 == holder, 0, 1))
    received = jnp.where(holder == core, rest[place_in], far[place_in])
    return jnp.where((ahead == 0) & (low == 0), head[jnp.where(mine, 0, 1)], received)


def gather_window(lead, head):
    beside = place(lead, lambda y, z, x, low, core: (y, z, x, 1 - low, core))
    sides = place(head, lambda y, z, x, low, core: (y, z, x + 1 - 2 * core, low, core))
    opposite = place(head, lambda y, z, x, low, core: (y, z, x + 2, low ^ core, core))
    corners = place(head, lambda y, z, x, low, core: (y, z, x - 1 + 2 * core, 1 - low, core))
    return jnp.concatenate([beside[None], sides, opposite, corners])


def contributions(items, out_shapes, prepared, window, after):
    def body(factor, trailing, limits, inverse, head, rest, far, after, *outs):
        for first in range(0, len(items), 2):
            group = items[first : first + 2]
            tiles = [destination(step, other) for step, other, _, _ in group]
            columns = [pl.ds(pl.multiple_of(tile * TILE, TILE), TILE) for tile in tiles]
            weights = []
            for tile in tiles:
                rows = window_piece(tile, head, rest, far)
                weights.append(
                    lax.dot_general(
                        rows, inverse[...], (((1,), (1,)), ((), ())), preferred_element_type=F32
                    ).astype(BF16)
                )
            weight = jnp.concatenate(weights, axis=0)
            for pair in range(TILES_DEV // 2):
                update = lax.dot_general(
                    factor[pair * 2 * TILE : (pair + 1) * 2 * TILE, :], weight,
                    (((1,), (1,)), ((), ())), preferred_element_type=F32,
                )
                for k in (2 * pair, 2 * pair + 1):
                    rows = slice(k * TILE, (k + 1) * TILE)
                    inner = (k % 2) * TILE
                    for m, (_, _, out, lead) in enumerate(group):
                        part = update[inner : inner + TILE, m * TILE : (m + 1) * TILE]
                        part = jnp.where(limits[k : k + 1, :] > tiles[m], part, 0.0)
                        value = (trailing[rows, columns[m]].astype(F32) - part).astype(BF16)
                        outs[out][(*lead, rows, slice(None))] = value

    here = pl.BlockSpec(memory_space=pltpu.VMEM)
    return pl.pallas_call(
        body,
        out_shape=[jax.ShapeDtypeStruct(shape, BF16) for shape in out_shapes],
        in_specs=[here] * 8,
        out_specs=[here] * len(out_shapes),
        compiler_params=pltpu.CompilerParams(vmem_limit_bytes=VMEM_LIMIT),
        cost_estimate=pl.CostEstimate(
            flops=2 * ROWS_DEV * PW * TILE * len(items),
            bytes_accessed=(PW + 2 * len(items) * TILE) * ROWS_DEV * 2,
            transcendentals=0,
        ),
    )(*prepared, *window, after)


def order_kernel(maps, trailing, ordered, limits):
    for t in range(TILES_DEV):
        target = pl.ds(pl.multiple_of(maps[0, t] * TILE, TILE), TILE)
        ordered[target, :] = trailing[t * TILE : (t + 1) * TILE, :]
        limits[pl.ds(maps[0, t], 1), :] = jnp.full((1, TILE), maps[0, TILES_DEV + t], jnp.int32)


def solve_kernel(maps, a21, inverse, out, factor, kept):
    out[...] = lax.dot_general(
        a21[...], inverse[...], (((1,), (1,)), ((), ())), preferred_element_type=F32
    ).astype(BF16)
    kept[...] = inverse[...]
    for t in range(TILES_DEV):
        target = pl.ds(pl.multiple_of(maps[0, t] * TILE, TILE), TILE)
        factor[target, :] = out[t * TILE : (t + 1) * TILE, :]


def in_vmem(kernel, flops, out_shape, maps, *operands):
    here = pl.BlockSpec(memory_space=pltpu.VMEM)
    return pl.pallas_call(
        kernel,
        out_shape=out_shape,
        in_specs=[pl.BlockSpec(memory_space=pltpu.SMEM)] + [here] * len(operands),
        out_specs=[here] * len(out_shape),
        compiler_params=pltpu.CompilerParams(vmem_limit_bytes=VMEM_LIMIT),
        cost_estimate=pl.CostEstimate(
            flops=flops, bytes_accessed=4 * 1024 * 1024, transcendentals=0
        ),
    )(maps, *operands)


def order(maps, trailing):
    shapes = [
        jax.ShapeDtypeStruct(trailing.shape, BF16),
        jax.ShapeDtypeStruct((TILES_DEV, TILE), jnp.int32),
    ]
    return in_vmem(order_kernel, 0, shapes, maps, trailing)


def solve(maps, a21, inverse):
    shapes = [jax.ShapeDtypeStruct(value.shape, BF16) for value in (a21, a21, inverse)]
    return in_vmem(solve_kernel, 2 * ROWS_DEV * PW * PW, shapes, maps, a21, inverse)


def add(*terms):
    total = terms[0].astype(F32)
    for term in terms[1:]:
        total = total + term.astype(F32)
    return total


def on_device(a21, l11_inv, a22, tasks, emap, parent_in):
    a21, l11_inv, a22 = a21[0], l11_inv[0], a22[0]
    lead = a21[:TILE]
    maps = jnp.concatenate([emap, tasks], axis=1)
    head, maps, a22 = lax.optimization_barrier((jnp.stack([lead, to_sibling(lead)]), maps, a22))
    rest = gather_window(lead, head)
    ordered, limits = order(maps, a22)
    rest, ordered, a21, l11_inv = lax.optimization_barrier((rest, ordered, a21, l11_inv))
    l21, factor, inverse = solve(maps, a21, l11_inv)
    prepared = factor, ordered, limits, inverse
    window = (head, rest, to_sibling(rest))

    def run(items, shapes, after):
        return contributions(items, shapes, prepared, window, after)

    one, two = (ROWS_DEV, TILE), (2, ROWS_DEV, TILE)
    def bf16(*terms):
        return add(*terms).astype(BF16)

    far, far_y = run([(4, 0, 0, ()), (4, 1, 1, ())], [one, one], prepared[0])
    up4, down4_y = along(far, 1), along(far_y, -1)
    (near1,) = run([(1, 1, 0, (0,)), (-1, 1, 0, (1,))], [two], far)
    next_y, next_ = run([(3, 1, 0, ()), (-3, 0, 1, ())], [one, one], near1)
    near1 = across_y(near1)
    up3_y, down3 = along(next_y, 1), along(next_, -1)
    up3, down3_y, near0 = run([(3, 0, 0, ()), (-3, 1, 1, ()), (0, 1, 2, ())], [one] * 3, next_y)
    up = along(bf16(up3, up4), 1)
    down3_y = bf16(down3_y, down4_y)
    down_y = along(down3_y, -1)
    up2_y, down2, up2, down2_y = run(
        [(2, 1, 0, ()), (-2, 0, 1, ()), (2, 0, 2, ()), (-2, 1, 3, ())], [one] * 4, down3_y
    )
    up_y = along_y(bf16(up2_y, up3_y), 1)
    down = along(bf16(down2, down3), -1)
    up1, own0 = run([(1, 0, 0, ()), (0, 0, 1, ())], [one] * 2, up2)
    up = along(bf16(up2, up), 1)
    down_y = along_y(bf16(down2_y, down_y), -1)
    up_y, near0 = lax.optimization_barrier((up_y, near0))
    near0 = across_y(near0)
    up = along(bf16(up1, up, up_y, near1[0]), 1)
    (down1,) = run([(-1, 0, 0, ())], [one], down_y)
    down = along(bf16(down1, down, down_y, near1[1]), -1)
    arrivals = add(own0, near0, up, down)
    return (l21[None], parent_in + arrivals)


def solution(mesh):
    return jax.shard_map(
        on_device,
        mesh=mesh,
        in_specs=(
            P("leaf", "panel", None),
            P("leaf", None, None),
            P("leaf", "panel", None),
            P("leaf", "panel"),
            P("leaf", "panel"),
            P("panel", "leaf"),
        ),
        out_specs=(P("leaf", "panel", None), P("panel", "leaf")),
        check_vma=False,
    )
```
